32 devices in a mesh: seq: 16 (over z, x, core), wsh: 2 (over y).
Axes of the slice: x: 2, y: 2, z: 4, core: 2. Of those that a mesh axis runs over, the one named last changes fastest.
Arguments:
- tokens: bfloat16 [8, 2048, 640], P('wsh', 'seq'), may hold values from -6 to 6
- group_offset: int32 [8, 16], P('wsh', 'seq'), may hold values from 0 to 1920, as said below
- q_weight: bfloat16 [2, 1024, 640], P(None, ('seq', 'wsh')), may hold values from -0.25 to 0.25
- k_weight: bfloat16 [2, 256, 640], P(None, ('seq', 'wsh')), may hold values from -0.25 to 0.25
- v_weight: bfloat16 [2, 256, 640], P(None, ('seq', 'wsh')), may hold values from -0.25 to 0.25
- o_weight: bfloat16 [2, 1024, 640], P(None, ('seq', 'wsh')), may hold values from -0.1875 to 0.1875
- gate_weight: bfloat16 [2, 2048, 640], P(None, ('seq', 'wsh')), may hold values from -0.25 to 0.25
- up_weight: bfloat16 [2, 2048, 640], P(None, ('seq', 'wsh')), may hold values from -0.25 to 0.25
- down_weight: bfloat16 [2, 2048, 640], P(None, ('seq', 'wsh')), may hold values from -0.125 to 0.125
- norm_gains: float32 [2, 4, 640], replicated, may hold values from 0.1 to 1.9
- head_gains: float32 [2, 2, 256], replicated, may hold values from 0.1 to 1.9
- out_grad: bfloat16 [8, 2048, 640], P('wsh', 'seq'), may hold values from -6 to 6
Outputs:
- block_out: bfloat16 [8, 2048, 640], P('wsh', 'seq')
- input_grad: float32 [8, 2048, 640], P('wsh', 'seq')
- q_grad: float32 [2, 1024, 640], P(None, ('seq', 'wsh'))
- k_grad: float32 [2, 256, 640], P(None, ('seq', 'wsh'))
- v_grad: float32 [2, 256, 640], P(None, ('seq', 'wsh'))
- o_grad: float32 [2, 1024, 640], P(None, ('seq', 'wsh'))
- gate_grad: float32 [2, 2048, 640], P(None, ('seq', 'wsh'))
- up_grad: float32 [2, 2048, 640], P(None, ('seq', 'wsh'))
- down_grad: float32 [2, 2048, 640], P(None, ('seq', 'wsh'))
- norm_grad: float32 [2, 4, 640], replicated
- head_grad: float32 [2, 2, 256], replicated
The draws below stay inside these ranges and needn't reach their ends.
Inputs may be any that keep to these rules, and one draw needn't show every extreme that they name: `group_offset`: each row is one sequence or two laid end to end; every sequence starts at a multiple of 128, so a value is 128 times the group's index within its sequence; the first group of each row has 0. Among the 4 rows of each index of wsh, one is a single sequence.
All inputs are finite; a program needn't handle non-finite values.
Results may differ from the reference program's by a relative error of at most 0.028.
Values may be sent and summed in bfloat16 or wider, within the bound.
A program may use at most 192 MiB of HBM per device.

```python
import jax
import jax.numpy as jnp
from jax import lax

D = 640
HQ = 4
HD = 256
FF = 2048
WINDOW = 512
LAYERS = 2
SEQ_DEV = 4
GROUP = 128
TOTAL = 2048
SEQS = 8
N_SEQ = 16


def draw_group_offset(key, part):
    key = jax.random.fold_in(key, 7)
    split_key, pick_key = jax.random.split(key)
    split_at = jax.random.randint(split_key, (SEQS,), 1, N_SEQ).astype(jnp.int32)
    chosen_row = jax.random.randint(pick_key, (SEQS // SEQ_DEV,), 0, SEQ_DEV).astype(jnp.int32)
    single_row = jnp.arange(SEQS, dtype=jnp.int32) % SEQ_DEV == jnp.repeat(chosen_row, SEQ_DEV, total_repeat_length=SEQS)
    split_at = jnp.where(single_row, N_SEQ, split_at)
    columns = jnp.arange(N_SEQ, dtype=jnp.int32)[None, :]
    group_index = jnp.where(columns < split_at[:, None], columns, columns - split_at[:, None])
    return (group_index * GROUP).astype(jnp.int32)


def block_scale(key, dims, cuts, least, high):
    factor_of = 1.0
    for dim, blocks in cuts:
        steps = jax.random.uniform(jax.random.fold_in(jax.random.fold_in(key, 6), dim), (blocks,), jnp.float32, least / len(cuts), high / len(cuts))
        factor_of = factor_of * jnp.repeat(jnp.exp(steps), dims[dim] // blocks).reshape((-1,) + (1,) * (len(dims) - 1 - dim))
    return factor_of


def centred(rng, shape, scale, bound, cuts=(), held_as=jnp.bfloat16):
    array = scale * jax.random.normal(rng, shape, jnp.float32)
    if cuts:
        array = array * block_scale(rng, shape, cuts, -0.22, 0.18)
    return jnp.clip(array, -bound, bound).astype(held_as)


def setup_inputs(seed: int = 0) -> dict:
    key_of = jax.random.split(jax.random.key(seed), 13)
    return {
        "tokens": centred(key_of[0], (SEQS, TOTAL, D), 1.0, 6.0, ((0, 2), (1, 16))),
        "group_offset": draw_group_offset(jax.random.fold_in(key_of[12], 71), 0),
        "q_weight": centred(key_of[2], (LAYERS, HQ * HD, D), D ** -0.5, 0.25, ((1, 32),)),
        "k_weight": centred(key_of[3], (LAYERS, HD, D), D ** -0.5, 0.25, ((1, 32),)),
        "v_weight": centred(key_of[4], (LAYERS, HD, D), D ** -0.5, 0.25, ((1, 32),)),
        "o_weight": centred(key_of[5], (LAYERS, HQ * HD, D), (HQ * HD) ** -0.5, 0.1875, ((1, 32),)),
        "gate_weight": centred(key_of[6], (LAYERS, FF, D), D ** -0.5, 0.25, ((1, 32),)),
        "up_weight": centred(key_of[7], (LAYERS, FF, D), D ** -0.5, 0.25, ((1, 32),)),
        "down_weight": centred(key_of[8], (LAYERS, FF, D), FF ** -0.5, 0.125, ((1, 32),)),
        "norm_gains": jnp.clip(1.0 + 0.18 * jax.random.normal(key_of[9], (LAYERS, 4, D), jnp.float32), 0.1, 1.9),
        "head_gains": jnp.clip(1.0 + 0.18 * jax.random.normal(key_of[10], (LAYERS, 2, HD), jnp.float32), 0.1, 1.9),
        "out_grad": centred(key_of[11], (SEQS, TOTAL, D), 1.0, 6.0, ((0, 2), (1, 16))),
    }


EPSILON = 1e-06
ROPE_BASE = 10000.0
MASKED = -1e+30
HIGHEST_PRECISION = lax.Precision.HIGHEST

@jax.custom_vjp
def low(v):
    return lax.optimization_barrier(v.astype(jnp.bfloat16)).astype(jnp.float32)

@jax.custom_vjp
def low_back(v):
    return v

def low_keep(v):
    return (low(v), None)

def low_pass(kept, grad):
    return (grad,)

def back_keep(v):
    return (v, None)

def back_low(kept, grad):
    return (low(grad),)
low.defvjp(low_keep, low_pass)
low_back.defvjp(back_keep, back_low)

def norm_gain(values, scaling):
    return values * lax.rsqrt(lax.optimization_barrier(jnp.mean(values * values, axis=-1, keepdims=True)) + EPSILON) * scaling

def rotate(values, angles):
    half_width = values.shape[-1] // 2
    leading = values[..., :half_width]
    trailing = values[..., half_width:]
    cosine = jnp.cos(angles)
    sine_part = jnp.sin(angles)
    return jnp.concatenate([leading * cosine - trailing * sine_part, trailing * cosine + leading * sine_part], axis=-1)

def frequencies(head_width):
    indices = jnp.arange(head_width // 2).astype(jnp.float32)
    return ROPE_BASE ** (-2.0 * indices / head_width)

def project(rows, matrix):
    return jnp.dot(rows, matrix.T, precision=HIGHEST_PRECISION)

def attention(rotated_query, k_rot, v_val, position):
    k_pad = jnp.concatenate([jnp.zeros((WINDOW, HD), jnp.float32), k_rot], axis=0)
    v_pad = jnp.concatenate([jnp.zeros((WINDOW, HD), jnp.float32), v_val], axis=0)

    def one_block(block_idx):
        start = (block_idx * WINDOW).astype(jnp.int32)
        queries = lax.dynamic_slice_in_dim(rotated_query, start, WINDOW, 0)
        key_matrix_rows = lax.dynamic_slice_in_dim(k_pad, start, 2 * WINDOW, 0)
        value_matrix_rows = lax.dynamic_slice_in_dim(v_pad, start, 2 * WINDOW, 0)
        places = lax.dynamic_slice_in_dim(position, start, WINDOW, 0)
        attention_scores = low_back(jnp.einsum('qhd,kd->hqk', queries, key_matrix_rows, precision=HIGHEST_PRECISION))
        distance = (jnp.arange(WINDOW)[:, None] + WINDOW - jnp.arange(2 * WINDOW)[None, :]).astype(jnp.int32)
        allowed = (distance >= 0) & (distance < WINDOW) & (distance <= places[:, None])
        attention_scores = jnp.where(allowed[None], attention_scores, MASKED)
        row_max = lax.optimization_barrier(jnp.max(attention_scores, axis=-1, keepdims=True))
        exped = jnp.exp(attention_scores - row_max)
        attention_probabilities = exped / lax.optimization_barrier(jnp.sum(exped, axis=-1, keepdims=True))
        return jnp.einsum('hqk,kd->qhd', low(attention_probabilities), value_matrix_rows, precision=HIGHEST_PRECISION)
    blocks = lax.map(jax.checkpoint(one_block), jnp.arange(TOTAL // WINDOW, dtype=jnp.int32))
    return blocks.reshape(TOTAL, HQ * HD)

def run_layer(stream, mats, gains, head_gain, position, angles):
    q_mat, k_mat, v_mat, o_mat, gate_mat, up_mat, down_mat = mats
    normed = low(norm_gain(stream, gains[0]))
    q_lin = low_back(project(normed, q_mat)).reshape(TOTAL, HQ, HD)
    k_lin = low_back(project(normed, k_mat))
    v_val = low(low_back(project(normed, v_mat)))
    rotated_query = low(rotate(norm_gain(q_lin, head_gain[0]), angles[:, None, :]) * HD ** (-0.5))
    k_rot = low(rotate(norm_gain(k_lin, head_gain[1]), angles))
    mixed = low_back(low(attention(rotated_query, k_rot, v_val, position)))
    attn_out = low_back(jnp.dot(mixed, o_mat, precision=HIGHEST_PRECISION))
    after_attn = stream + norm_gain(attn_out, gains[1])
    hidden = low(norm_gain(after_attn, gains[2]))
    gate_pre = low_back(project(hidden, gate_mat))
    up_pre = low_back(project(hidden, up_mat))
    activated = low(jax.nn.gelu(gate_pre, approximate=True) * up_pre)
    down_out = low_back(jnp.dot(activated, down_mat, precision=HIGHEST_PRECISION))
    return after_attn + norm_gain(down_out, gains[3])

def reference(tokens, group_offset, q_weight, k_weight, v_weight, o_weight, gate_weight, up_weight, down_weight, norm_gains, head_gains, out_grad):
    params = (q_weight.astype(jnp.float32), k_weight.astype(jnp.float32), v_weight.astype(jnp.float32), o_weight.astype(jnp.float32), gate_weight.astype(jnp.float32), up_weight.astype(jnp.float32), down_weight.astype(jnp.float32), norm_gains.astype(jnp.float32), head_gains.astype(jnp.float32))
    local_index = (jnp.arange(TOTAL) % GROUP).astype(jnp.int32)

    def row_step(grad_sums, row_inputs):
        row_tokens, row_offset, row_grad = row_inputs
        position = (jnp.repeat(row_offset, GROUP, total_repeat_length=TOTAL).astype(jnp.int32) + local_index).astype(jnp.int32)
        angles = position.astype(jnp.float32)[:, None] * frequencies(HD)[None, :]

        def forward(stream, weights):
            for layer_idx in range(LAYERS):
                mats = tuple((matrix[layer_idx] for matrix in weights[:7]))
                stream = run_layer(stream, mats, weights[7][layer_idx], weights[8][layer_idx], position, angles)
            return stream
        result, pullback = jax.vjp(forward, row_tokens.astype(jnp.float32), params)
        input_part, weight_parts = pullback(row_grad.astype(jnp.float32))
        grad_sums = jax.tree.map(lambda total_part, new_part: total_part + new_part, grad_sums, weight_parts)
        return (grad_sums, (result.astype(jnp.bfloat16), input_part))
    zero_grads = jax.tree.map(jnp.zeros_like, params)
    grad_sums, (block_out, input_grad) = lax.scan(row_step, zero_grads, (tokens, group_offset, out_grad))
    return (block_out, input_grad, grad_sums[0], grad_sums[1], grad_sums[2], grad_sums[3], grad_sums[4], grad_sums[5], grad_sums[6], grad_sums[7], grad_sums[8])
```

```python
import jax
import jax.numpy as jnp
from jax import lax
from jax.sharding import PartitionSpec as P

WINDOW = 512


EPSILON = 1e-06
ROPE_BASE = 10000.0
MASKED = -1e30


def shifted(value, axis, steps):
    count = lax.axis_size(axis)
    initial, last = (max(0, -steps), min(count, count - steps))
    return lax.ppermute(value, axis, [(source, source + steps) for source in range(initial, last)])


def norm_gain(values, scaling):
    return values * lax.rsqrt(jnp.mean(values * values, axis=-1, keepdims=True) + EPSILON) * scaling


def rotate(values, angles):
    half_width = values.shape[-1] // 2
    leading = values[..., :half_width]
    trailing = values[..., half_width:]
    cosine, sine_part = angles
    return jnp.concatenate(
        [leading * cosine - trailing * sine_part, trailing * cosine + leading * sine_part], axis=-1
    )


def frequencies(head_width):
    indices = jnp.arange(head_width // 2).astype(jnp.float32)
    return ROPE_BASE ** (-2.0 * indices / head_width)


def gelu_product(gate_in, up_in):
    return jax.nn.gelu(gate_in, approximate=True) * up_in


def query_rot(q_lin, head_gain, angles, head_count):
    shaped = q_lin.reshape(q_lin.shape[0], q_lin.shape[1], head_count, -1)
    return rotate(
        norm_gain(shaped, head_gain), tuple(part[:, :, None, :] for part in angles)
    ) * shaped.shape[-1] ** (-0.5)


def key_rot(k_lin, head_gain, angles):
    return rotate(norm_gain(k_lin, head_gain), angles)


def device_index():
    return lax.axis_index("seq") * lax.axis_size("wsh") + lax.axis_index("wsh")


def bits_of(size, unit):
    found = []
    step = 1
    while step < size:
        found.insert(0, step * unit)
        step *= 2
    return found


def exchange_plan():
    wsh_count = lax.axis_size("wsh")
    seq_bits = bits_of(lax.axis_size("seq"), wsh_count)
    wsh_bits = bits_of(wsh_count, 1)
    core_bit = seq_bits[-1]
    near_bit = seq_bits[-2:-1]
    far_bits = seq_bits[:-2]
    orders = (far_bits + wsh_bits + near_bit, near_bit + far_bits + wsh_bits)
    return core_bit, orders, far_bits + near_bit, wsh_bits


def flip(value, bit_of_core):
    core_bit = exchange_plan()[0]
    count = lax.axis_size("seq") * lax.axis_size("wsh")
    pairs = [(d, d ^ bit_of_core[1 if d & core_bit else 0]) for d in range(count)]
    return lax.ppermute(value, ("seq", "wsh"), pairs)


def my_bit(bit_of_core):
    me = device_index()
    core = (me & exchange_plan()[0]) != 0
    return jnp.where(core, me & bit_of_core[1], me & bit_of_core[0]) != 0


def is_upper_core():
    return (device_index() & exchange_plan()[0]) != 0


def gather_blocks(block, ordered, axis):
    core_bit, orders, upper_bits, wsh_bits = exchange_plan()
    held = jnp.expand_dims(block, axis)
    for pair in zip(*orders):
        came = flip(held, pair)
        if ordered:
            swap = my_bit(pair)
            held = jnp.concatenate(
                [jnp.where(swap, came, held), jnp.where(swap, held, came)], axis=axis
            )
        else:
            held = jnp.concatenate([held, came], axis=axis)
    came = flip(held, (core_bit, core_bit))
    if not ordered:
        return jnp.concatenate([held, came], axis=axis)
    upper = is_upper_core()
    halves = (jnp.where(upper, came, held), jnp.where(upper, held, came))
    target = upper_bits + wsh_bits
    placed = []
    for half, order in zip(halves, orders):
        split = half.reshape((2,) * len(order) + half.shape[1:])
        stored = order[::-1]
        trailing = tuple(range(len(order), split.ndim))
        placed.append(split.transpose(tuple(stored.index(bit) for bit in target) + trailing))
    whole = jnp.stack(placed, axis=len(upper_bits))
    return whole.reshape((-1,) + block.shape)


def add_terms(kept, came):
    return kept.astype(jnp.float32) + came.astype(jnp.float32)


def scatter_blocks(blocks, ordered, axis):
    core_bit, orders, upper_bits, wsh_bits = exchange_plan()
    if ordered:
        target = upper_bits + wsh_bits
        split = blocks.reshape((2,) * (len(target) + 1) + blocks.shape[1:])
        parts = []
        for core, order in enumerate(orders):
            half = lax.index_in_dim(split, core, len(upper_bits), keepdims=False)
            trailing = tuple(range(len(order), half.ndim))
            half = half.transpose(tuple(target.index(bit) for bit in order[::-1]) + trailing)
            parts.append(half.reshape((-1,) + blocks.shape[1:]))
        upper = is_upper_core()
        kept = jnp.where(upper, parts[1], parts[0])
        sent = jnp.where(upper, parts[0], parts[1])
    else:
        kept, sent = jnp.split(blocks, 2, axis=axis)
    total = add_terms(kept, flip(sent, (core_bit, core_bit)))
    for pair in list(zip(*orders))[::-1]:
        total = total.astype(jnp.bfloat16)
        kept, sent = jnp.split(total, 2, axis=axis)
        if ordered:
            swap = my_bit(pair)
            kept, sent = (jnp.where(swap, sent, kept), jnp.where(swap, kept, sent))
        total = add_terms(kept, flip(sent, pair))
    return jnp.squeeze(total, axis)


def sum_all(value):
    core_bit, orders, upper_bits, wsh_bits = exchange_plan()
    for bit in [core_bit] + upper_bits[::-1] + wsh_bits:
        value = value + flip(value, (bit, bit))
    return value


def layer_weights(weights, layer_idx):
    rows = [member[layer_idx] for member in weights]
    attn = gather_blocks(jnp.concatenate(rows[:4], axis=0), True, 0)
    ffn = gather_blocks(jnp.stack(rows[4:]), False, 1)
    mats = []
    start = 0
    for member in rows[:4]:
        mats.append(attn[:, start : start + member.shape[0]].reshape(-1, member.shape[1]))
        start += member.shape[0]
    for kind in range(3):
        mats.append(ffn[kind].reshape(-1, ffn.shape[-1]))
    return tuple(mats)


def share_attn(grads):
    count = lax.axis_size("seq") * lax.axis_size("wsh")
    shaped = [
        member.astype(jnp.bfloat16).reshape(count, -1, member.shape[1]) for member in grads
    ]
    summed = scatter_blocks(jnp.concatenate(shaped, axis=1), True, 0)
    shares = []
    start = 0
    for member in shaped:
        shares.append(summed[start : start + member.shape[1]])
        start += member.shape[1]
    return shares


def share_ffn(grads):
    count = lax.axis_size("seq") * lax.axis_size("wsh")
    stacked = jnp.stack(
        [member.astype(jnp.bfloat16).reshape(count, -1, member.shape[1]) for member in grads]
    )
    summed = scatter_blocks(stacked, False, 1)
    return [summed[kind] for kind in range(3)]


def share_grads(grads):
    return tuple(share_attn(grads[:4]) + share_ffn(grads[4:]))


def earlier_keys(packed_tokens, hop_count):
    pieces = [shifted(packed_tokens, "seq", hop) for hop in range(hop_count, 0, -1)]
    return jnp.concatenate(pieces + [packed_tokens], axis=1)


def returned_grads(grad_all, hop_count, group_len):
    summed = grad_all[:, hop_count * group_len :]
    for hop in range(hop_count, 0, -1):
        start = (hop_count - hop) * group_len
        piece = grad_all[:, start : start + group_len].astype(jnp.bfloat16)
        summed = summed + shifted(piece, "seq", -hop).astype(jnp.float32)
    return summed


def masked_scores(rotated_query, key_matrix_rows, allowed):
    attention_scores = jnp.einsum(
        "uzmt,upt->umzp", rotated_query, key_matrix_rows, preferred_element_type=jnp.float32
    )
    return jnp.where(allowed[:, None], attention_scores, MASKED)


def forward_layer(stream, gathered, gains, head_gain, angles, allowed, hop_count):
    q_mat, k_mat, v_mat, o_mat, gate_mat, up_mat, down_mat = gathered
    head_width = head_gain.shape[-1]
    head_count = q_mat.shape[0] // head_width
    batch_rows, group_len = (stream.shape[0], stream.shape[1])
    normed = norm_gain(stream, gains[0]).astype(jnp.bfloat16)
    q_lin = jnp.einsum("bcd,ed->bce", normed, q_mat, preferred_element_type=jnp.float32)
    k_lin = jnp.einsum("bcd,ed->bce", normed, k_mat, preferred_element_type=jnp.float32)
    v_val = jnp.einsum("bcd,ed->bce", normed, v_mat, preferred_element_type=jnp.float32).astype(
        jnp.bfloat16
    )
    rotated_query = query_rot(q_lin, head_gain[0], angles, head_count).astype(jnp.bfloat16)
    k_rot = key_rot(k_lin, head_gain[1], angles).astype(jnp.bfloat16)
    packed_tokens = earlier_keys(jnp.concatenate([k_rot, v_val], axis=-1), hop_count)
    attention_scores = masked_scores(rotated_query, packed_tokens[..., :head_width], allowed)
    row_max = jnp.max(attention_scores, axis=-1, keepdims=True)
    log_total = row_max + jnp.log(
        jnp.sum(jnp.exp(attention_scores - row_max), axis=-1, keepdims=True)
    )
    probabilities_bfloat = jnp.exp(attention_scores - log_total).astype(jnp.bfloat16)
    mixed = jnp.einsum(
        "faln,fnv->flav",
        probabilities_bfloat,
        packed_tokens[..., head_width:],
        preferred_element_type=jnp.float32,
    )
    mixed = mixed.reshape(batch_rows, group_len, head_count * head_width).astype(jnp.bfloat16)
    attn_out = jnp.einsum("bce,ed->bcd", mixed, o_mat, preferred_element_type=jnp.float32)
    after_attn = stream + norm_gain(attn_out, gains[1])
    hidden = norm_gain(after_attn, gains[2]).astype(jnp.bfloat16)
    gate_pre = jnp.einsum("bcd,fd->bcf", hidden, gate_mat, preferred_element_type=jnp.float32)
    up_pre = jnp.einsum("bcd,fd->bcf", hidden, up_mat, preferred_element_type=jnp.float32)
    activated = gelu_product(gate_pre, up_pre).astype(jnp.bfloat16)
    down_out = jnp.einsum("bcf,fd->bcd", activated, down_mat, preferred_element_type=jnp.float32)
    layer_out = after_attn + norm_gain(down_out, gains[3])
    saved = (
        stream,
        normed,
        q_lin,
        k_lin,
        rotated_query,
        packed_tokens,
        log_total,
        mixed,
        attn_out,
        after_attn,
        hidden,
        gate_pre,
        up_pre,
        activated,
        down_out,
    )
    return (saved, layer_out)


def backward_layer(upstream, saved, gathered, gains, head_gain, angles, allowed, hop_count):
    (
        stream,
        normed,
        q_lin,
        k_lin,
        rotated_query,
        packed_tokens,
        log_total,
        mixed,
        attn_out,
        after_attn,
        hidden,
        gate_pre,
        up_pre,
        activated,
        down_out,
    ) = saved
    q_mat, k_mat, v_mat, o_mat, gate_mat, up_mat, down_mat = gathered
    head_width = head_gain.shape[-1]
    head_count = q_mat.shape[0] // head_width
    batch_rows, group_len = (stream.shape[0], stream.shape[1])
    unused, pullback = jax.vjp(norm_gain, down_out, gains[3])
    d_down, g_post_ff = pullback(upstream)
    d_down = d_down.astype(jnp.bfloat16)
    dw_down = jnp.einsum("bcf,bcd->fd", activated, d_down, preferred_element_type=jnp.float32)
    d_act = jnp.einsum("bcd,fd->bcf", d_down, down_mat, preferred_element_type=jnp.float32)
    unused, pullback = jax.vjp(gelu_product, gate_pre, up_pre)
    d_gate, d_up = pullback(d_act)
    d_gate = d_gate.astype(jnp.bfloat16)
    d_up = d_up.astype(jnp.bfloat16)
    dw_gate = jnp.einsum("bcf,bcd->fd", d_gate, hidden, preferred_element_type=jnp.float32)
    dw_up = jnp.einsum("bcf,bcd->fd", d_up, hidden, preferred_element_type=jnp.float32)
    d_hidden = jnp.einsum(
        "bcf,fd->bcd", d_gate, gate_mat, preferred_element_type=jnp.float32
    ) + jnp.einsum("bcf,fd->bcd", d_up, up_mat, preferred_element_type=jnp.float32)
    unused, pullback = jax.vjp(norm_gain, after_attn, gains[2])
    d_after, g_pre_ff = pullback(d_hidden)
    d_after = upstream + d_after
    unused, pullback = jax.vjp(norm_gain, attn_out, gains[1])
    d_attn, g_post_attn = pullback(d_after)
    d_attn = d_attn.astype(jnp.bfloat16)
    dw_output = jnp.einsum("bce,bcd->ed", mixed, d_attn, preferred_element_type=jnp.float32)
    mixed_gradient = jnp.einsum(
        "bcd,ed->bce", d_attn, o_mat, preferred_element_type=jnp.float32
    ).astype(jnp.bfloat16)
    mixed_gradient = mixed_gradient.reshape(batch_rows, group_len, head_count, head_width)
    key_matrix_rows = packed_tokens[..., :head_width]
    value_matrix_rows = packed_tokens[..., head_width:]
    attention_probabilities = jnp.exp(
        masked_scores(rotated_query, key_matrix_rows, allowed) - log_total
    )
    probability_gradient = jnp.einsum(
        "uzmt,upt->umzp", mixed_gradient, value_matrix_rows, preferred_element_type=jnp.float32
    )
    score_gradient = (
        attention_probabilities
        * (
            probability_gradient
            - jnp.sum(probability_gradient * attention_probabilities, axis=-1, keepdims=True)
        )
    ).astype(jnp.bfloat16)
    rotated_query_gradient = jnp.einsum(
        "faln,fnv->flav", score_gradient, key_matrix_rows, preferred_element_type=jnp.float32
    )
    key_gradient_rows = jnp.einsum(
        "tznj,tnzq->tjq", score_gradient, rotated_query, preferred_element_type=jnp.float32
    )
    d_values = jnp.einsum(
        "tznj,tnzq->tjq",
        attention_probabilities.astype(jnp.bfloat16),
        mixed_gradient,
        preferred_element_type=jnp.float32,
    )
    d_packed = returned_grads(
        jnp.concatenate([key_gradient_rows, d_values], axis=-1), hop_count, group_len
    )

    def query_part(lin_rows, gain_row):
        return query_rot(lin_rows, gain_row, angles, head_count)

    def key_part(lin_rows, gain_row):
        return key_rot(lin_rows, gain_row, angles)

    unused, pullback = jax.vjp(query_part, q_lin, head_gain[0])
    d_qlin, g_query = pullback(rotated_query_gradient)
    unused, pullback = jax.vjp(key_part, k_lin, head_gain[1])
    d_klin, g_key = pullback(d_packed[..., :head_width])
    d_query = d_qlin.astype(jnp.bfloat16)
    d_key = d_klin.astype(jnp.bfloat16)
    d_value = d_packed[..., head_width:].astype(jnp.bfloat16)
    dw_query = jnp.einsum("bce,bcd->ed", d_query, normed, preferred_element_type=jnp.float32)
    dw_key = jnp.einsum("bce,bcd->ed", d_key, normed, preferred_element_type=jnp.float32)
    dw_value = jnp.einsum("bce,bcd->ed", d_value, normed, preferred_element_type=jnp.float32)
    d_normed = (
        jnp.einsum("bce,ed->bcd", d_query, q_mat, preferred_element_type=jnp.float32)
        + jnp.einsum("bce,ed->bcd", d_key, k_mat, preferred_element_type=jnp.float32)
        + jnp.einsum("bce,ed->bcd", d_value, v_mat, preferred_element_type=jnp.float32)
    )
    unused, pullback = jax.vjp(norm_gain, stream, gains[0])
    d_stream, g_pre_attn = pullback(d_normed)
    d_stream = d_after + d_stream
    grads = (dw_query, dw_key, dw_value, dw_output, dw_gate, dw_up, dw_down)
    return (
        d_stream,
        grads,
        jnp.stack([g_pre_attn, g_post_attn, g_pre_ff, g_post_ff]),
        jnp.stack([g_query, g_key]),
    )


def body(
    tokens,
    group_offset,
    q_weight,
    k_weight,
    v_weight,
    o_weight,
    gate_weight,
    up_weight,
    down_weight,
    norm_gains,
    head_gains,
    out_grad,
):
    group_len = tokens.shape[1]
    layer_count = q_weight.shape[0]
    head_width = head_gains.shape[-1]
    hop_count = WINDOW // group_len
    position = group_offset + jnp.arange(group_len, dtype=jnp.int32)[None, :]
    angles = position.astype(jnp.float32)[..., None] * frequencies(head_width)[None, None, :]
    angles = lax.optimization_barrier((jnp.cos(angles), jnp.sin(angles)))
    key_span = (hop_count + 1) * group_len
    distance = (
        jnp.arange(group_len, dtype=jnp.int32)[:, None]
        + hop_count * group_len
        - jnp.arange(key_span, dtype=jnp.int32)[None, :]
    )
    allowed = (
        (distance[None] >= 0) & (distance[None] < WINDOW) & (distance[None] <= position[:, :, None])
    )
    weights = (q_weight, k_weight, v_weight, o_weight, gate_weight, up_weight, down_weight)
    stream = tokens.astype(jnp.float32)
    records = []
    for layer_idx in range(layer_count):
        gathered = layer_weights(weights, layer_idx)
        saved, stream = forward_layer(
            stream,
            gathered,
            norm_gains[layer_idx],
            head_gains[layer_idx],
            angles,
            allowed,
            hop_count,
        )
        records.append((saved, gathered))
    block_out = stream.astype(jnp.bfloat16)
    upstream = out_grad.astype(jnp.float32)
    weight_shares = [None] * layer_count
    norm_parts = [None] * layer_count
    head_parts = [None] * layer_count
    for layer_idx in range(layer_count - 1, -1, -1):
        saved, kept_mats = records[layer_idx]
        gathered = kept_mats
        upstream, grads, norm_part, head_part = backward_layer(
            upstream,
            saved,
            gathered,
            norm_gains[layer_idx],
            head_gains[layer_idx],
            angles,
            allowed,
            hop_count,
        )
        weight_shares[layer_idx] = share_grads(grads)
        norm_parts[layer_idx] = norm_part
        head_parts[layer_idx] = head_part
    totals = [None] * layer_count
    for layer_idx in range(layer_count - 1, -1, -1):
        flat = jnp.concatenate(
            [norm_parts[layer_idx].reshape(-1), head_parts[layer_idx].reshape(-1)]
        )
        totals[layer_idx] = sum_all(flat.reshape(-1, 128))
    both = jnp.stack(totals).reshape(layer_count, -1)
    norm_size = norm_gains[0].size
    norm_total = both[:, :norm_size].reshape(norm_gains.shape)
    head_total = both[:, norm_size:].reshape(head_gains.shape)
    stacked = tuple(
        (
            jnp.stack([weight_shares[layer_idx][member] for layer_idx in range(layer_count)])
            for member in range(7)
        )
    )
    return (block_out, upstream) + stacked + (norm_total, head_total)


def solution(mesh):
    in_specs = (
        P("wsh", "seq", None),
        P("wsh", "seq"),
        P(None, ("seq", "wsh"), None),
        P(None, ("seq", "wsh"), None),
        P(None, ("seq", "wsh"), None),
        P(None, ("seq", "wsh"), None),
        P(None, ("seq", "wsh"), None),
        P(None, ("seq", "wsh"), None),
        P(None, ("seq", "wsh"), None),
        P(),
        P(),
        P("wsh", "seq", None),
    )
    out_specs = (
        P("wsh", "seq", None),
        P("wsh", "seq", None),
        P(None, ("seq", "wsh"), None),
        P(None, ("seq", "wsh"), None),
        P(None, ("seq", "wsh"), None),
        P(None, ("seq", "wsh"), None),
        P(None, ("seq", "wsh"), None),
        P(None, ("seq", "wsh"), None),
        P(None, ("seq", "wsh"), None),
        P(),
        P(),
    )
    return jax.shard_map(body, mesh=mesh, in_specs=in_specs, out_specs=out_specs, check_vma=False)
```

```python
import jax
import jax.numpy as jnp
from jax import lax
from jax.sharding import PartitionSpec as P

WINDOW = 512


EPSILON = 1e-06
ROPE_BASE = 10000.0
MASKED = -1e30


def shifted(value, axis, steps):
    count = lax.axis_size(axis)
    initial, last = (max(0, -steps), min(count, count - steps))
    return lax.ppermute(value, axis, [(source, source + steps) for source in range(initial, last)])


def norm_gain(values, scaling):
    return values * lax.rsqrt(jnp.mean(values * values, axis=-1, keepdims=True) + EPSILON) * scaling


def rotate(values, angles):
    half_width = values.shape[-1] // 2
    leading = values[..., :half_width]
    trailing = values[..., half_width:]
    cosine, sine_part = angles
    return jnp.concatenate(
        [leading * cosine - trailing * sine_part, trailing * cosine + leading * sine_part], axis=-1
    )


def frequencies(head_width):
    indices = jnp.arange(head_width // 2).astype(jnp.float32)
    return ROPE_BASE ** (-2.0 * indices / head_width)


def gelu_product(gate_in, up_in):
    return jax.nn.gelu(gate_in, approximate=True) * up_in


def query_rot(q_lin, head_gain, angles, head_count):
    shaped = q_lin.reshape(q_lin.shape[0], q_lin.shape[1], head_count, -1)
    return rotate(
        norm_gain(shaped, head_gain), tuple(part[:, :, None, :] for part in angles)
    ) * shaped.shape[-1] ** (-0.5)


def key_rot(k_lin, head_gain, angles):
    return rotate(norm_gain(k_lin, head_gain), angles)


def device_index():
    return lax.axis_index("seq") * lax.axis_size("wsh") + lax.axis_index("wsh")


def bits_of(size, unit):
    found = []
    step = 1
    while step < size:
        found.insert(0, step * unit)
        step *= 2
    return found


def exchange_plan():
    wsh_count = lax.axis_size("wsh")
    seq_bits = bits_of(lax.axis_size("seq"), wsh_count)
    wsh_bits = bits_of(wsh_count, 1)
    core_bit = seq_bits[-1]
    near_bit = seq_bits[-2:-1]
    far_bits = seq_bits[:-2]
    orders = (far_bits + wsh_bits + near_bit, near_bit + far_bits + wsh_bits)
    return core_bit, orders, far_bits + near_bit, wsh_bits


def flip(value, bit_of_core):
    core_bit = exchange_plan()[0]
    count = lax.axis_size("seq") * lax.axis_size("wsh")
    pairs = [(d, d ^ bit_of_core[1 if d & core_bit else 0]) for d in range(count)]
    return lax.ppermute(value, ("seq", "wsh"), pairs)


def my_bit(bit_of_core):
    me = device_index()
    core = (me & exchange_plan()[0]) != 0
    return jnp.where(core, me & bit_of_core[1], me & bit_of_core[0]) != 0


def is_upper_core():
    return (device_index() & exchange_plan()[0]) != 0


class Transfer:
    def __init__(self, steps):
        self.steps = steps
        self.result = None
        self.flying = next(steps)

    def push(self, came):
        try:
            self.flying = self.steps.send(came)
        except StopIteration as stop:
            self.flying = None
            self.result = stop.value

    def finish(self):
        while self.flying is not None:
            self.push(self.flying)
        return self.result


def advance(values, transfers):
    live = [transfer for transfer in transfers if transfer.flying is not None]
    if not live:
        return values
    values, came = lax.optimization_barrier((values, [transfer.flying for transfer in live]))
    for transfer, arrived in zip(live, came):
        transfer.push(arrived)
    return values


def gather_blocks(block, ordered, axis):
    core_bit, orders, upper_bits, wsh_bits = exchange_plan()
    held = jnp.expand_dims(block, axis)
    for pair in zip(*orders):
        came = yield flip(held, pair)
        if ordered:
            swap = my_bit(pair)
            held = jnp.concatenate(
                [jnp.where(swap, came, held), jnp.where(swap, held, came)], axis=axis
            )
        else:
            held = jnp.concatenate([held, came], axis=axis)
    came = yield flip(held, (core_bit, core_bit))
    if not ordered:
        return jnp.concatenate([held, came], axis=axis)
    upper = is_upper_core()
    halves = (jnp.where(upper, came, held), jnp.where(upper, held, came))
    target = upper_bits + wsh_bits
    placed = []
    for half, order in zip(halves, orders):
        split = half.reshape((2,) * len(order) + half.shape[1:])
        stored = order[::-1]
        trailing = tuple(range(len(order), split.ndim))
        placed.append(split.transpose(tuple(stored.index(bit) for bit in target) + trailing))
    whole = jnp.stack(placed, axis=len(upper_bits))
    return whole.reshape((-1,) + block.shape)


def add_terms(kept, came):
    return kept.astype(jnp.float32) + came.astype(jnp.float32)


def scatter_blocks(blocks, ordered, axis):
    core_bit, orders, upper_bits, wsh_bits = exchange_plan()
    if ordered:
        target = upper_bits + wsh_bits
        split = blocks.reshape((2,) * (len(target) + 1) + blocks.shape[1:])
        parts = []
        for core, order in enumerate(orders):
            half = lax.index_in_dim(split, core, len(upper_bits), keepdims=False)
            trailing = tuple(range(len(order), half.ndim))
            half = half.transpose(tuple(target.index(bit) for bit in order[::-1]) + trailing)
            parts.append(half.reshape((-1,) + blocks.shape[1:]))
        upper = is_upper_core()
        kept = jnp.where(upper, parts[1], parts[0])
        sent = jnp.where(upper, parts[0], parts[1])
    else:
        kept, sent = jnp.split(blocks, 2, axis=axis)
    came = yield flip(sent, (core_bit, core_bit))
    total = add_terms(kept, came)
    for pair in list(zip(*orders))[::-1]:
        total = total.astype(jnp.bfloat16)
        kept, sent = jnp.split(total, 2, axis=axis)
        if ordered:
            swap = my_bit(pair)
            kept, sent = (jnp.where(swap, sent, kept), jnp.where(swap, kept, sent))
        came = yield flip(sent, pair)
        total = add_terms(kept, came)
    return jnp.squeeze(total, axis)


def sum_all(value):
    core_bit, orders, upper_bits, wsh_bits = exchange_plan()
    for bit in [core_bit] + upper_bits[::-1] + wsh_bits:
        value = value + flip(value, (bit, bit))
    return value


def attn_gather(rows):
    return Transfer(gather_blocks(jnp.concatenate(rows, axis=0), True, 0))


def attn_mats(whole, rows):
    mats = []
    start = 0
    for member in rows:
        mats.append(whole[:, start : start + member.shape[0]].reshape(-1, member.shape[1]))
        start += member.shape[0]
    return mats


def ffn_gather(rows):
    return Transfer(gather_blocks(jnp.stack(rows), False, 1))


def ffn_mats(whole):
    return [whole[kind].reshape(-1, whole.shape[-1]) for kind in range(whole.shape[0])]


def device_blocks(grads):
    count = lax.axis_size("seq") * lax.axis_size("wsh")
    return [member.astype(jnp.bfloat16).reshape(count, -1, member.shape[1]) for member in grads]


def attn_scatter(grads):
    return Transfer(scatter_blocks(jnp.concatenate(device_blocks(grads), axis=1), True, 0))


def attn_shares(summed, rows):
    shares = []
    start = 0
    for member in rows:
        shares.append(summed[start : start + member.shape[0]])
        start += member.shape[0]
    return shares


def ffn_scatter(grads):
    return Transfer(scatter_blocks(jnp.stack(device_blocks(grads)), False, 1))


def earlier_keys(packed_tokens, hop_count):
    pieces = [shifted(packed_tokens, "seq", hop) for hop in range(hop_count, 0, -1)]
    return jnp.concatenate(pieces + [packed_tokens], axis=1)


def returned_grads(grad_all, hop_count, group_len):
    summed = grad_all[:, hop_count * group_len :]
    for hop in range(hop_count, 0, -1):
        start = (hop_count - hop) * group_len
        piece = grad_all[:, start : start + group_len].astype(jnp.bfloat16)
        summed = summed + shifted(piece, "seq", -hop).astype(jnp.float32)
    return summed


def masked_scores(rotated_query, key_matrix_rows, allowed):
    attention_scores = jnp.einsum(
        "uzmt,upt->umzp", rotated_query, key_matrix_rows, preferred_element_type=jnp.float32
    )
    return jnp.where(allowed[:, None], attention_scores, MASKED)


def forward_layer(
    stream, attn_weights, ffn_weights, gains, head_gain, angles, allowed, hop_count, tick
):
    q_mat, k_mat, v_mat, o_mat = attn_weights
    head_width = head_gain.shape[-1]
    head_count = q_mat.shape[0] // head_width
    batch_rows, group_len = (stream.shape[0], stream.shape[1])
    normed = norm_gain(stream, gains[0]).astype(jnp.bfloat16)
    q_lin = jnp.einsum("bcd,ed->bce", normed, q_mat, preferred_element_type=jnp.float32)
    k_lin = jnp.einsum("bcd,ed->bce", normed, k_mat, preferred_element_type=jnp.float32)
    v_val = jnp.einsum("bcd,ed->bce", normed, v_mat, preferred_element_type=jnp.float32).astype(
        jnp.bfloat16
    )
    rotated_query = query_rot(q_lin, head_gain[0], angles, head_count).astype(jnp.bfloat16)
    k_rot = key_rot(k_lin, head_gain[1], angles).astype(jnp.bfloat16)
    rotated_query, k_rot, v_val = tick("projected", (rotated_query, k_rot, v_val))
    packed_tokens = earlier_keys(jnp.concatenate([k_rot, v_val], axis=-1), hop_count)
    attention_scores = masked_scores(rotated_query, packed_tokens[..., :head_width], allowed)
    row_max = jnp.max(attention_scores, axis=-1, keepdims=True)
    log_total = row_max + jnp.log(
        jnp.sum(jnp.exp(attention_scores - row_max), axis=-1, keepdims=True)
    )
    probabilities_bfloat = jnp.exp(attention_scores - log_total).astype(jnp.bfloat16)
    mixed = jnp.einsum(
        "faln,fnv->flav",
        probabilities_bfloat,
        packed_tokens[..., head_width:],
        preferred_element_type=jnp.float32,
    )
    mixed = mixed.reshape(batch_rows, group_len, head_count * head_width).astype(jnp.bfloat16)
    mixed = tick("mixed", mixed)
    attn_out = jnp.einsum("bce,ed->bcd", mixed, o_mat, preferred_element_type=jnp.float32)
    after_attn = stream + norm_gain(attn_out, gains[1])
    hidden = norm_gain(after_attn, gains[2]).astype(jnp.bfloat16)
    after_attn, hidden = tick("hidden", (after_attn, hidden))
    gate_mat, up_mat, down_mat = ffn_weights()
    gate_pre = jnp.einsum("bcd,fd->bcf", hidden, gate_mat, preferred_element_type=jnp.float32)
    up_pre = jnp.einsum("bcd,fd->bcf", hidden, up_mat, preferred_element_type=jnp.float32)
    activated = gelu_product(gate_pre, up_pre).astype(jnp.bfloat16)
    activated = tick("activated", activated)
    down_out = jnp.einsum("bcf,fd->bcd", activated, down_mat, preferred_element_type=jnp.float32)
    layer_out = tick("layer_out", after_attn + norm_gain(down_out, gains[3]))
    saved = (
        stream,
        normed,
        q_lin,
        k_lin,
        rotated_query,
        packed_tokens,
        log_total,
        mixed,
        attn_out,
        after_attn,
        hidden,
        gate_pre,
        up_pre,
        activated,
        down_out,
    )
    return (saved, (q_mat, k_mat, v_mat, o_mat, gate_mat, up_mat, down_mat), layer_out)


def backward_layer(
    upstream, saved, gathered, gains, head_gain, angles, allowed, hop_count, tick, send_ffn, send_attn
):
    (
        stream,
        normed,
        q_lin,
        k_lin,
        rotated_query,
        packed_tokens,
        log_total,
        mixed,
        attn_out,
        after_attn,
        hidden,
        gate_pre,
        up_pre,
        activated,
        down_out,
    ) = saved
    q_mat, k_mat, v_mat, o_mat, gate_mat, up_mat, down_mat = gathered
    head_width = head_gain.shape[-1]
    head_count = q_mat.shape[0] // head_width
    batch_rows, group_len = (stream.shape[0], stream.shape[1])
    unused, pullback = jax.vjp(norm_gain, down_out, gains[3])
    d_down, g_post_ff = pullback(upstream)
    d_down = d_down.astype(jnp.bfloat16)
    dw_down = jnp.einsum("bcf,bcd->fd", activated, d_down, preferred_element_type=jnp.float32)
    d_act = jnp.einsum("bcd,fd->bcf", d_down, down_mat, preferred_element_type=jnp.float32)
    unused, pullback = jax.vjp(gelu_product, gate_pre, up_pre)
    d_gate, d_up = pullback(d_act)
    d_gate = d_gate.astype(jnp.bfloat16)
    d_up = d_up.astype(jnp.bfloat16)
    d_gate, d_up = tick("d_gate", (d_gate, d_up))
    dw_gate = jnp.einsum("bcf,bcd->fd", d_gate, hidden, preferred_element_type=jnp.float32)
    dw_up = jnp.einsum("bcf,bcd->fd", d_up, hidden, preferred_element_type=jnp.float32)
    d_hidden = jnp.einsum(
        "bcf,fd->bcd", d_gate, gate_mat, preferred_element_type=jnp.float32
    ) + jnp.einsum("bcf,fd->bcd", d_up, up_mat, preferred_element_type=jnp.float32)
    d_hidden = tick("d_hidden", d_hidden)
    send_ffn((dw_gate, dw_up, dw_down))
    unused, pullback = jax.vjp(norm_gain, after_attn, gains[2])
    d_after, g_pre_ff = pullback(d_hidden)
    d_after = upstream + d_after
    unused, pullback = jax.vjp(norm_gain, attn_out, gains[1])
    d_attn, g_post_attn = pullback(d_after)
    d_attn = d_attn.astype(jnp.bfloat16)
    dw_output = jnp.einsum("bce,bcd->ed", mixed, d_attn, preferred_element_type=jnp.float32)
    mixed_gradient = jnp.einsum(
        "bcd,ed->bce", d_attn, o_mat, preferred_element_type=jnp.float32
    ).astype(jnp.bfloat16)
    mixed_gradient = tick("d_mixed", mixed_gradient)
    mixed_gradient = mixed_gradient.reshape(batch_rows, group_len, head_count, head_width)
    key_matrix_rows = packed_tokens[..., :head_width]
    value_matrix_rows = packed_tokens[..., head_width:]
    attention_probabilities = jnp.exp(
        masked_scores(rotated_query, key_matrix_rows, allowed) - log_total
    )
    probability_gradient = jnp.einsum(
        "uzmt,upt->umzp", mixed_gradient, value_matrix_rows, preferred_element_type=jnp.float32
    )
    score_gradient = (
        attention_probabilities
        * (
            probability_gradient
            - jnp.sum(probability_gradient * attention_probabilities, axis=-1, keepdims=True)
        )
    ).astype(jnp.bfloat16)
    rotated_query_gradient = jnp.einsum(
        "faln,fnv->flav", score_gradient, key_matrix_rows, preferred_element_type=jnp.float32
    )
    key_gradient_rows = jnp.einsum(
        "tznj,tnzq->tjq", score_gradient, rotated_query, preferred_element_type=jnp.float32
    )
    d_values = jnp.einsum(
        "tznj,tnzq->tjq",
        attention_probabilities.astype(jnp.bfloat16),
        mixed_gradient,
        preferred_element_type=jnp.float32,
    )
    d_packed = jnp.concatenate([key_gradient_rows, d_values], axis=-1)
    d_packed, rotated_query_gradient = tick("d_packed", (d_packed, rotated_query_gradient))
    d_packed = returned_grads(d_packed, hop_count, group_len)

    def query_part(lin_rows, gain_row):
        return query_rot(lin_rows, gain_row, angles, head_count)

    def key_part(lin_rows, gain_row):
        return key_rot(lin_rows, gain_row, angles)

    unused, pullback = jax.vjp(query_part, q_lin, head_gain[0])
    d_qlin, g_query = pullback(rotated_query_gradient)
    unused, pullback = jax.vjp(key_part, k_lin, head_gain[1])
    d_klin, g_key = pullback(d_packed[..., :head_width])
    d_query = d_qlin.astype(jnp.bfloat16)
    d_key = d_klin.astype(jnp.bfloat16)
    d_value = d_packed[..., head_width:].astype(jnp.bfloat16)
    dw_query = jnp.einsum("bce,bcd->ed", d_query, normed, preferred_element_type=jnp.float32)
    dw_key = jnp.einsum("bce,bcd->ed", d_key, normed, preferred_element_type=jnp.float32)
    dw_value = jnp.einsum("bce,bcd->ed", d_value, normed, preferred_element_type=jnp.float32)
    d_normed = (
        jnp.einsum("bce,ed->bcd", d_query, q_mat, preferred_element_type=jnp.float32)
        + jnp.einsum("bce,ed->bcd", d_key, k_mat, preferred_element_type=jnp.float32)
        + jnp.einsum("bce,ed->bcd", d_value, v_mat, preferred_element_type=jnp.float32)
    )
    unused, pullback = jax.vjp(norm_gain, stream, gains[0])
    d_stream, g_pre_attn = pullback(d_normed)
    d_stream = tick("d_stream", d_after + d_stream)
    send_attn((dw_query, dw_key, dw_value, dw_output))
    return (
        d_stream,
        jnp.stack([g_pre_attn, g_post_attn, g_pre_ff, g_post_ff]),
        jnp.stack([g_query, g_key]),
    )


def body(
    tokens,
    group_offset,
    q_weight,
    k_weight,
    v_weight,
    o_weight,
    gate_weight,
    up_weight,
    down_weight,
    norm_gains,
    head_gains,
    out_grad,
):
    group_len = tokens.shape[1]
    layer_count = q_weight.shape[0]
    head_width = head_gains.shape[-1]
    hop_count = WINDOW // group_len
    position = group_offset + jnp.arange(group_len, dtype=jnp.int32)[None, :]
    angles = position.astype(jnp.float32)[..., None] * frequencies(head_width)[None, None, :]
    angles = lax.optimization_barrier((jnp.cos(angles), jnp.sin(angles)))
    key_span = (hop_count + 1) * group_len
    distance = (
        jnp.arange(group_len, dtype=jnp.int32)[:, None]
        + hop_count * group_len
        - jnp.arange(key_span, dtype=jnp.int32)[None, :]
    )
    allowed = (
        (distance[None] >= 0) & (distance[None] < WINDOW) & (distance[None] <= position[:, :, None])
    )
    weights = (q_weight, k_weight, v_weight, o_weight, gate_weight, up_weight, down_weight)
    stream = tokens.astype(jnp.float32)
    attn_rows = [[member[layer_idx] for member in weights[:4]] for layer_idx in range(layer_count)]
    ffn_rows = [[member[layer_idx] for member in weights[4:]] for layer_idx in range(layer_count)]
    attn_moves = [None] * layer_count
    ffn_moves = [None] * layer_count
    attn_moves[0] = attn_gather(attn_rows[0])
    ffn_moves[0] = ffn_gather(ffn_rows[0])
    attn_moves[0].finish()
    for early in range(3):
        ffn_moves[0].push(ffn_moves[0].flying)
    records = []
    for layer_idx in range(layer_count):
        following = layer_idx + 1 if layer_idx + 1 < layer_count else None

        def tick(stage, values, layer_idx=layer_idx, following=following):
            moves = []
            if stage in ("projected", "mixed", "hidden"):
                moves.append(ffn_moves[layer_idx])
            if following is not None:
                if stage == "projected":
                    values, fresh = lax.optimization_barrier((values, attn_rows[following]))
                    attn_moves[following] = attn_gather(fresh)
                elif stage == "mixed":
                    attn_moves[following].push(attn_moves[following].flying)
                    moves.append(attn_moves[following])
                elif stage == "hidden":
                    moves.append(attn_moves[following])
                    values, fresh = lax.optimization_barrier((values, ffn_rows[following]))
                    ffn_moves[following] = ffn_gather(fresh)
                else:
                    moves.append(attn_moves[following])
                    moves.append(ffn_moves[following])
            return advance(values, moves)

        def ffn_weights(layer_idx=layer_idx):
            return ffn_mats(ffn_moves[layer_idx].finish())

        saved, gathered, stream = forward_layer(
            stream,
            attn_mats(attn_moves[layer_idx].finish(), attn_rows[layer_idx]),
            ffn_weights,
            norm_gains[layer_idx],
            head_gains[layer_idx],
            angles,
            allowed,
            hop_count,
            tick,
        )
        records.append((saved, gathered))
    block_out = stream.astype(jnp.bfloat16)
    upstream = out_grad.astype(jnp.float32)
    norm_parts = [None] * layer_count
    head_parts = [None] * layer_count
    attn_sums = [None] * layer_count
    ffn_sums = [None] * layer_count
    sums = []

    def back_tick(stage, values):
        return advance(values, sums)

    for layer_idx in range(layer_count - 1, -1, -1):
        saved, gathered = records[layer_idx]

        def send_ffn(grads, layer_idx=layer_idx):
            ffn_sums[layer_idx] = ffn_scatter(grads)
            sums.append(ffn_sums[layer_idx])

        def send_attn(grads, layer_idx=layer_idx):
            attn_sums[layer_idx] = attn_scatter(grads)
            sums.append(attn_sums[layer_idx])

        upstream, norm_parts[layer_idx], head_parts[layer_idx] = backward_layer(
            upstream,
            saved,
            gathered,
            norm_gains[layer_idx],
            head_gains[layer_idx],
            angles,
            allowed,
            hop_count,
            back_tick,
            send_ffn,
            send_attn,
        )
    weight_shares = []
    for layer_idx in range(layer_count):
        ffn_total = ffn_sums[layer_idx].finish()
        weight_shares.append(
            attn_shares(attn_sums[layer_idx].finish(), attn_rows[layer_idx])
            + [ffn_total[kind] for kind in range(3)]
        )
    flat = jnp.concatenate([jnp.stack(norm_parts).reshape(-1), jnp.stack(head_parts).reshape(-1)])
    both = sum_all(flat.reshape(-1, 128)).reshape(-1)
    norm_total = both[: norm_gains.size].reshape(norm_gains.shape)
    head_total = both[norm_gains.size :].reshape(head_gains.shape)
    stacked = tuple(
        (
            jnp.stack([weight_shares[layer_idx][member] for layer_idx in range(layer_count)])
            for member in range(7)
        )
    )
    return (block_out, upstream) + stacked + (norm_total, head_total)


def solution(mesh):
    in_specs = (
        P("wsh", "seq", None),
        P("wsh", "seq"),
        P(None, ("seq", "wsh"), None),
        P(None, ("seq", "wsh"), None),
        P(None, ("seq", "wsh"), None),
        P(None, ("seq", "wsh"), None),
        P(None, ("seq", "wsh"), None),
        P(None, ("seq", "wsh"), None),
        P(None, ("seq", "wsh"), None),
        P(),
        P(),
        P("wsh", "seq", None),
    )
    out_specs = (
        P("wsh", "seq", None),
        P("wsh", "seq", None),
        P(None, ("seq", "wsh"), None),
        P(None, ("seq", "wsh"), None),
        P(None, ("seq", "wsh"), None),
        P(None, ("seq", "wsh"), None),
        P(None, ("seq", "wsh"), None),
        P(None, ("seq", "wsh"), None),
        P(None, ("seq", "wsh"), None),
        P(),
        P(),
    )
    return jax.shard_map(body, mesh=mesh, in_specs=in_specs, out_specs=out_specs, check_vma=False)
```

```python
import jax
import jax.numpy as jnp
from jax import lax
from jax.sharding import PartitionSpec as P

WINDOW = 512


EPSILON = 1e-06
ROPE_BASE = 10000.0
MASKED = -1e30


def shifted(value, axis, steps):
    count = lax.axis_size(axis)
    initial, last = (max(0, -steps), min(count, count - steps))
    return lax.ppermute(value, axis, [(source, source + steps) for source in range(initial, last)])


def norm_gain(values, scaling):
    return values * lax.rsqrt(jnp.mean(values * values, axis=-1, keepdims=True) + EPSILON) * scaling


def rotate(values, angles):
    half_width = values.shape[-1] // 2
    leading = values[..., :half_width]
    trailing = values[..., half_width:]
    cosine, sine_part = angles
    return jnp.concatenate(
        [leading * cosine - trailing * sine_part, trailing * cosine + leading * sine_part], axis=-1
    )


def frequencies(head_width):
    indices = jnp.arange(head_width // 2).astype(jnp.float32)
    return ROPE_BASE ** (-2.0 * indices / head_width)


def gelu_product(gate_in, up_in):
    return jax.nn.gelu(gate_in, approximate=True) * up_in


def query_rot(q_lin, head_gain, angles, head_count):
    shaped = q_lin.reshape(q_lin.shape[0], q_lin.shape[1], head_count, -1)
    return rotate(
        norm_gain(shaped, head_gain), tuple(part[:, :, None, :] for part in angles)
    ) * shaped.shape[-1] ** (-0.5)


def key_rot(k_lin, head_gain, angles):
    return rotate(norm_gain(k_lin, head_gain), angles)


def device_index():
    return lax.axis_index("seq") * lax.axis_size("wsh") + lax.axis_index("wsh")


def bits_of(size, unit):
    found = []
    step = 1
    while step < size:
        found.insert(0, step * unit)
        step *= 2
    return found


def exchange_plan():
    wsh_count = lax.axis_size("wsh")
    seq_bits = bits_of(lax.axis_size("seq"), wsh_count)
    wsh_bits = bits_of(wsh_count, 1)
    core_bit = seq_bits[-1]
    near_bit = seq_bits[-2:-1]
    far_bits = seq_bits[:-2]
    orders = (far_bits + wsh_bits + near_bit, near_bit + far_bits + wsh_bits)
    return core_bit, orders, far_bits + near_bit, wsh_bits


def flip(value, bit_of_core):
    core_bit = exchange_plan()[0]
    count = lax.axis_size("seq") * lax.axis_size("wsh")
    pairs = [(d, d ^ bit_of_core[1 if d & core_bit else 0]) for d in range(count)]
    return lax.ppermute(value, ("seq", "wsh"), pairs)


def my_bit(bit_of_core):
    me = device_index()
    core = (me & exchange_plan()[0]) != 0
    return jnp.where(core, me & bit_of_core[1], me & bit_of_core[0]) != 0


def is_upper_core():
    return (device_index() & exchange_plan()[0]) != 0


class Transfer:
    def __init__(self, steps):
        self.steps = steps
        self.result = None
        self.flying = next(steps)

    def push(self, came):
        try:
            self.flying = self.steps.send(came)
        except StopIteration as stop:
            self.flying = None
            self.result = stop.value

    def finish(self):
        while self.flying is not None:
            self.push(self.flying)
        return self.result


def advance(values, transfers):
    live = [transfer for transfer in transfers if transfer.flying is not None]
    if not live:
        return values
    values, came = lax.optimization_barrier((values, [transfer.flying for transfer in live]))
    for transfer, arrived in zip(live, came):
        transfer.push(arrived)
    return values


def gather_blocks(block, ordered, axis):
    core_bit, orders, upper_bits, wsh_bits = exchange_plan()
    held = jnp.expand_dims(block, axis)
    for pair in zip(*orders):
        came = yield flip(held, pair)
        if ordered:
            swap = my_bit(pair)
            held = jnp.concatenate(
                [jnp.where(swap, came, held), jnp.where(swap, held, came)], axis=axis
            )
        else:
            held = jnp.concatenate([held, came], axis=axis)
    came = yield flip(held, (core_bit, core_bit))
    if not ordered:
        return jnp.concatenate([held, came], axis=axis)
    upper = is_upper_core()
    halves = (jnp.where(upper, came, held), jnp.where(upper, held, came))
    target = upper_bits + wsh_bits
    placed = []
    for half, order in zip(halves, orders):
        split = half.reshape((2,) * len(order) + half.shape[1:])
        stored = order[::-1]
        trailing = tuple(range(len(order), split.ndim))
        placed.append(split.transpose(tuple(stored.index(bit) for bit in target) + trailing))
    whole = jnp.stack(placed, axis=len(upper_bits))
    return whole.reshape((-1,) + block.shape)


def add_terms(kept, came):
    return kept.astype(jnp.float32) + came.astype(jnp.float32)


def scatter_blocks(blocks, ordered, axis):
    core_bit, orders, upper_bits, wsh_bits = exchange_plan()
    if ordered:
        target = upper_bits + wsh_bits
        split = blocks.reshape((2,) * (len(target) + 1) + blocks.shape[1:])
        parts = []
        for core, order in enumerate(orders):
            half = lax.index_in_dim(split, core, len(upper_bits), keepdims=False)
            trailing = tuple(range(len(order), half.ndim))
            half = half.transpose(tuple(target.index(bit) for bit in order[::-1]) + trailing)
            parts.append(half.reshape((-1,) + blocks.shape[1:]))
        upper = is_upper_core()
        kept = jnp.where(upper, parts[1], parts[0])
        sent = jnp.where(upper, parts[0], parts[1])
    else:
        kept, sent = jnp.split(blocks, 2, axis=axis)
    came = yield flip(sent, (core_bit, core_bit))
    total = add_terms(kept, came)
    for pair in list(zip(*orders))[::-1]:
        total = total.astype(jnp.bfloat16)
        kept, sent = jnp.split(total, 2, axis=axis)
        if ordered:
            swap = my_bit(pair)
            kept, sent = (jnp.where(swap, sent, kept), jnp.where(swap, kept, sent))
        came = yield flip(sent, pair)
        total = add_terms(kept, came)
    return jnp.squeeze(total, axis)


def sum_all(value):
    core_bit, orders, upper_bits, wsh_bits = exchange_plan()
    for bit in [core_bit] + upper_bits[::-1] + wsh_bits:
        came = yield flip(value, (bit, bit))
        value = value + came
    return value


def attn_gather(rows):
    return Transfer(gather_blocks(jnp.concatenate(rows, axis=0), True, 0))


def attn_mats(whole, rows):
    mats = []
    start = 0
    for member in rows:
        mats.append(whole[:, start : start + member.shape[0]].reshape(-1, member.shape[1]))
        start += member.shape[0]
    return mats


def ffn_gather(rows):
    return Transfer(gather_blocks(jnp.stack(rows), False, 1))


def ffn_mats(whole):
    return [whole[kind].reshape(-1, whole.shape[-1]) for kind in range(whole.shape[0])]


def device_blocks(grads):
    count = lax.axis_size("seq") * lax.axis_size("wsh")
    return [member.astype(jnp.bfloat16).reshape(count, -1, member.shape[1]) for member in grads]


def attn_scatter(grads):
    return Transfer(scatter_blocks(jnp.concatenate(device_blocks(grads), axis=1), True, 0))


def attn_shares(summed, rows):
    shares = []
    start = 0
    for member in rows:
        shares.append(summed[start : start + member.shape[0]])
        start += member.shape[0]
    return shares


def ffn_scatter(grads):
    return Transfer(scatter_blocks(jnp.stack(device_blocks(grads)), False, 1))


def exchange_rows(blocks):
    count = blocks.shape[0]
    total = lax.axis_size("seq")
    place = lax.axis_index("seq") % count

    def by_distance(value):
        step = 1
        while step < count:
            swapped = jnp.stack([value[index ^ step] for index in range(count)])
            value = jnp.where((place & step) != 0, swapped, value)
            step *= 2
        return value

    outgoing = by_distance(blocks)
    arrived = [outgoing[0]]
    for step in range(1, count):
        pairs = [(source, source ^ step) for source in range(total)]
        arrived.append(lax.ppermute(outgoing[step], "seq", pairs))
    return by_distance(jnp.stack(arrived))


def context_blocks(packed_tokens, hop_count):
    group_count, group_len, width = packed_tokens.shape
    before = shifted(packed_tokens, "seq", group_count)
    line = jnp.concatenate([before, packed_tokens], axis=0).reshape(-1, width)
    span = (hop_count + 1) * group_len
    return jnp.stack(
        [line[group * group_len : group * group_len + span] for group in range(group_count)]
    )


def returned_grads(grad_all, hop_count, group_len):
    group_count = grad_all.shape[0]
    slots = [None] * (2 * group_count)
    for group in range(group_count):
        for hop in range(hop_count + 1):
            piece = grad_all[group, hop * group_len : (hop + 1) * group_len]
            slot = group + hop
            slots[slot] = piece if slots[slot] is None else slots[slot] + piece
    outgoing = jnp.stack(slots[:group_count]).astype(jnp.bfloat16)
    came = shifted(outgoing, "seq", -group_count)
    return jnp.stack(slots[group_count:]) + came.astype(jnp.float32)


def masked_scores(rotated_query, key_matrix_rows, allowed):
    attention_scores = jnp.einsum(
        "uzmt,upt->umzp", rotated_query, key_matrix_rows, preferred_element_type=jnp.float32
    )
    return jnp.where(allowed[:, None], attention_scores, MASKED)


def forward_layer(
    stream, attn_weights, ffn_weights, gains, head_gain, angles, allowed, hop_count, tick
):
    q_mat, k_mat, v_mat, o_mat = attn_weights
    head_width = head_gain.shape[-1]
    head_count = q_mat.shape[0] // head_width
    batch_rows, group_len = (stream.shape[0], stream.shape[1])
    normed = norm_gain(stream, gains[0]).astype(jnp.bfloat16)
    q_lin = jnp.einsum("bcd,ed->bce", normed, q_mat, preferred_element_type=jnp.float32)
    k_lin = jnp.einsum("bcd,ed->bce", normed, k_mat, preferred_element_type=jnp.float32)
    v_val = jnp.einsum("bcd,ed->bce", normed, v_mat, preferred_element_type=jnp.float32).astype(
        jnp.bfloat16
    )
    rotated_query = query_rot(q_lin, head_gain[0], angles, head_count).astype(jnp.bfloat16)
    k_rot = key_rot(k_lin, head_gain[1], angles).astype(jnp.bfloat16)
    rotated_query, k_rot, v_val = tick("projected", (rotated_query, k_rot, v_val))
    packed_tokens = context_blocks(jnp.concatenate([k_rot, v_val], axis=-1), hop_count)
    attention_scores = masked_scores(rotated_query, packed_tokens[..., :head_width], allowed)
    row_max = jnp.max(attention_scores, axis=-1, keepdims=True)
    log_total = row_max + jnp.log(
        jnp.sum(jnp.exp(attention_scores - row_max), axis=-1, keepdims=True)
    )
    probabilities_bfloat = jnp.exp(attention_scores - log_total).astype(jnp.bfloat16)
    mixed = jnp.einsum(
        "faln,fnv->flav",
        probabilities_bfloat,
        packed_tokens[..., head_width:],
        preferred_element_type=jnp.float32,
    )
    mixed = mixed.reshape(batch_rows, group_len, head_count * head_width).astype(jnp.bfloat16)
    mixed = tick("mixed", mixed)
    attn_out = jnp.einsum("bce,ed->bcd", mixed, o_mat, preferred_element_type=jnp.float32)
    after_attn = stream + norm_gain(attn_out, gains[1])
    hidden = norm_gain(after_attn, gains[2]).astype(jnp.bfloat16)
    after_attn, hidden = tick("hidden", (after_attn, hidden))
    gate_mat, up_mat, down_mat = ffn_weights()
    gate_pre = jnp.einsum("bcd,fd->bcf", hidden, gate_mat, preferred_element_type=jnp.float32)
    up_pre = jnp.einsum("bcd,fd->bcf", hidden, up_mat, preferred_element_type=jnp.float32)
    activated = gelu_product(gate_pre, up_pre).astype(jnp.bfloat16)
    activated = tick("activated", activated)
    down_out = jnp.einsum("bcf,fd->bcd", activated, down_mat, preferred_element_type=jnp.float32)
    layer_out = tick("layer_out", after_attn + norm_gain(down_out, gains[3]))
    saved = (
        stream,
        normed,
        q_lin,
        k_lin,
        rotated_query,
        packed_tokens,
        log_total,
        mixed,
        attn_out,
        after_attn,
        hidden,
        gate_pre,
        up_pre,
        activated,
        down_out,
    )
    return (saved, (q_mat, k_mat, v_mat, o_mat, gate_mat, up_mat, down_mat), layer_out)


def backward_layer(
    upstream, saved, gathered, gains, head_gain, angles, allowed, hop_count, tick, send_ffn, send_attn
):
    (
        stream,
        normed,
        q_lin,
        k_lin,
        rotated_query,
        packed_tokens,
        log_total,
        mixed,
        attn_out,
        after_attn,
        hidden,
        gate_pre,
        up_pre,
        activated,
        down_out,
    ) = saved
    q_mat, k_mat, v_mat, o_mat, gate_mat, up_mat, down_mat = gathered
    head_width = head_gain.shape[-1]
    head_count = q_mat.shape[0] // head_width
    batch_rows, group_len = (stream.shape[0], stream.shape[1])
    unused, pullback = jax.vjp(norm_gain, down_out, gains[3])
    d_down, g_post_ff = pullback(upstream)
    d_down = d_down.astype(jnp.bfloat16)
    dw_down = jnp.einsum("bcf,bcd->fd", activated, d_down, preferred_element_type=jnp.float32)
    d_act = jnp.einsum("bcd,fd->bcf", d_down, down_mat, preferred_element_type=jnp.float32)
    unused, pullback = jax.vjp(gelu_product, gate_pre, up_pre)
    d_gate, d_up = pullback(d_act)
    d_gate = d_gate.astype(jnp.bfloat16)
    d_up = d_up.astype(jnp.bfloat16)
    d_gate, d_up = tick("d_gate", (d_gate, d_up))
    dw_gate = jnp.einsum("bcf,bcd->fd", d_gate, hidden, preferred_element_type=jnp.float32)
    dw_up = jnp.einsum("bcf,bcd->fd", d_up, hidden, preferred_element_type=jnp.float32)
    d_hidden = jnp.einsum(
        "bcf,fd->bcd", d_gate, gate_mat, preferred_element_type=jnp.float32
    ) + jnp.einsum("bcf,fd->bcd", d_up, up_mat, preferred_element_type=jnp.float32)
    d_hidden = tick("d_hidden", d_hidden)
    send_ffn((dw_gate, dw_up, dw_down))
    unused, pullback = jax.vjp(norm_gain, after_attn, gains[2])
    d_after, g_pre_ff = pullback(d_hidden)
    d_after = upstream + d_after
    unused, pullback = jax.vjp(norm_gain, attn_out, gains[1])
    d_attn, g_post_attn = pullback(d_after)
    d_attn = d_attn.astype(jnp.bfloat16)
    dw_output = jnp.einsum("bce,bcd->ed", mixed, d_attn, preferred_element_type=jnp.float32)
    mixed_gradient = jnp.einsum(
        "bcd,ed->bce", d_attn, o_mat, preferred_element_type=jnp.float32
    ).astype(jnp.bfloat16)
    mixed_gradient = tick("d_mixed", mixed_gradient)
    mixed_gradient = mixed_gradient.reshape(batch_rows, group_len, head_count, head_width)
    key_matrix_rows = packed_tokens[..., :head_width]
    value_matrix_rows = packed_tokens[..., head_width:]
    attention_probabilities = jnp.exp(
        masked_scores(rotated_query, key_matrix_rows, allowed) - log_total
    )
    probability_gradient = jnp.einsum(
        "uzmt,upt->umzp", mixed_gradient, value_matrix_rows, preferred_element_type=jnp.float32
    )
    score_gradient = (
        attention_probabilities
        * (
            probability_gradient
            - jnp.sum(probability_gradient * attention_probabilities, axis=-1, keepdims=True)
        )
    ).astype(jnp.bfloat16)
    rotated_query_gradient = jnp.einsum(
        "faln,fnv->flav", score_gradient, key_matrix_rows, preferred_element_type=jnp.float32
    )
    key_gradient_rows = jnp.einsum(
        "tznj,tnzq->tjq", score_gradient, rotated_query, preferred_element_type=jnp.float32
    )
    d_values = jnp.einsum(
        "tznj,tnzq->tjq",
        attention_probabilities.astype(jnp.bfloat16),
        mixed_gradient,
        preferred_element_type=jnp.float32,
    )
    d_packed = jnp.concatenate([key_gradient_rows, d_values], axis=-1)
    d_packed, rotated_query_gradient = tick("d_packed", (d_packed, rotated_query_gradient))
    d_packed = returned_grads(d_packed, hop_count, group_len)

    def query_part(lin_rows, gain_row):
        return query_rot(lin_rows, gain_row, angles, head_count)

    def key_part(lin_rows, gain_row):
        return key_rot(lin_rows, gain_row, angles)

    unused, pullback = jax.vjp(query_part, q_lin, head_gain[0])
    d_qlin, g_query = pullback(rotated_query_gradient)
    unused, pullback = jax.vjp(key_part, k_lin, head_gain[1])
    d_klin, g_key = pullback(d_packed[..., :head_width])
    d_query = d_qlin.astype(jnp.bfloat16)
    d_key = d_klin.astype(jnp.bfloat16)
    d_value = d_packed[..., head_width:].astype(jnp.bfloat16)
    dw_query = jnp.einsum("bce,bcd->ed", d_query, normed, preferred_element_type=jnp.float32)
    dw_key = jnp.einsum("bce,bcd->ed", d_key, normed, preferred_element_type=jnp.float32)
    dw_value = jnp.einsum("bce,bcd->ed", d_value, normed, preferred_element_type=jnp.float32)
    d_normed = (
        jnp.einsum("bce,ed->bcd", d_query, q_mat, preferred_element_type=jnp.float32)
        + jnp.einsum("bce,ed->bcd", d_key, k_mat, preferred_element_type=jnp.float32)
        + jnp.einsum("bce,ed->bcd", d_value, v_mat, preferred_element_type=jnp.float32)
    )
    unused, pullback = jax.vjp(norm_gain, stream, gains[0])
    d_stream, g_pre_attn = pullback(d_normed)
    d_stream = tick("d_stream", d_after + d_stream)
    send_attn((dw_query, dw_key, dw_value, dw_output))
    return (
        d_stream,
        jnp.stack([g_pre_attn, g_post_attn, g_pre_ff, g_post_ff]),
        jnp.stack([g_query, g_key]),
    )


def body(
    tokens,
    group_offset,
    q_weight,
    k_weight,
    v_weight,
    o_weight,
    gate_weight,
    up_weight,
    down_weight,
    norm_gains,
    head_gains,
    out_grad,
):
    group_len = tokens.shape[1]
    layer_count = q_weight.shape[0]
    head_width = head_gains.shape[-1]
    hop_count = WINDOW // group_len
    marks = (group_offset // group_len).astype(tokens.dtype)
    marks = jnp.broadcast_to(marks[:, :, None], (tokens.shape[0], 16, tokens.shape[2]))
    tokens = exchange_rows(jnp.concatenate([tokens, marks], axis=1))
    group_offset = tokens[:, group_len, :1].astype(jnp.int32) * group_len
    tokens = tokens[:, :group_len]
    position = group_offset + jnp.arange(group_len, dtype=jnp.int32)[None, :]
    angles = position.astype(jnp.float32)[..., None] * frequencies(head_width)[None, None, :]
    angles = lax.optimization_barrier((jnp.cos(angles), jnp.sin(angles)))
    key_span = (hop_count + 1) * group_len
    distance = (
        jnp.arange(group_len, dtype=jnp.int32)[:, None]
        + hop_count * group_len
        - jnp.arange(key_span, dtype=jnp.int32)[None, :]
    )
    allowed = (
        (distance[None] >= 0) & (distance[None] < WINDOW) & (distance[None] <= position[:, :, None])
    )
    weights = (q_weight, k_weight, v_weight, o_weight, gate_weight, up_weight, down_weight)
    stream = tokens.astype(jnp.float32)
    attn_rows = [[member[layer_idx] for member in weights[:4]] for layer_idx in range(layer_count)]
    ffn_rows = [[member[layer_idx] for member in weights[4:]] for layer_idx in range(layer_count)]
    attn_moves = [None] * layer_count
    ffn_moves = [None] * layer_count
    attn_moves[0] = attn_gather(attn_rows[0])
    ffn_moves[0] = ffn_gather(ffn_rows[0])
    attn_moves[0].finish()
    for early in range(3):
        ffn_moves[0].push(ffn_moves[0].flying)
    records = []
    for layer_idx in range(layer_count):
        following = layer_idx + 1 if layer_idx + 1 < layer_count else None

        def tick(stage, values, layer_idx=layer_idx, following=following):
            moves = []
            if stage in ("projected", "mixed", "hidden"):
                moves.append(ffn_moves[layer_idx])
            if following is not None:
                if stage == "projected":
                    values, fresh = lax.optimization_barrier((values, attn_rows[following]))
                    attn_moves[following] = attn_gather(fresh)
                elif stage == "mixed":
                    attn_moves[following].push(attn_moves[following].flying)
                    moves.append(attn_moves[following])
                elif stage == "hidden":
                    moves.append(attn_moves[following])
                    values, fresh = lax.optimization_barrier((values, ffn_rows[following]))
                    ffn_moves[following] = ffn_gather(fresh)
                else:
                    moves.append(attn_moves[following])
                    moves.append(ffn_moves[following])
            return advance(values, moves)

        def ffn_weights(layer_idx=layer_idx):
            return ffn_mats(ffn_moves[layer_idx].finish())

        saved, gathered, stream = forward_layer(
            stream,
            attn_mats(attn_moves[layer_idx].finish(), attn_rows[layer_idx]),
            ffn_weights,
            norm_gains[layer_idx],
            head_gains[layer_idx],
            angles,
            allowed,
            hop_count,
            tick,
        )
        records.append((saved, gathered))
    block_out = exchange_rows(stream.astype(jnp.bfloat16))
    out_grad = exchange_rows(out_grad)
    upstream = out_grad.astype(jnp.float32)
    norm_parts = [None] * layer_count
    head_parts = [None] * layer_count
    attn_sums = [None] * layer_count
    ffn_sums = [None] * layer_count
    sums = []

    def back_tick(stage, values):
        return advance(values, sums)

    for layer_idx in range(layer_count - 1, -1, -1):
        saved, gathered = records[layer_idx]

        def send_ffn(grads, layer_idx=layer_idx):
            ffn_sums[layer_idx] = ffn_scatter(grads)
            sums.append(ffn_sums[layer_idx])

        def send_attn(grads, layer_idx=layer_idx):
            attn_sums[layer_idx] = attn_scatter(grads)
            sums.append(attn_sums[layer_idx])

        upstream, norm_parts[layer_idx], head_parts[layer_idx] = backward_layer(
            upstream,
            saved,
            gathered,
            norm_gains[layer_idx],
            head_gains[layer_idx],
            angles,
            allowed,
            hop_count,
            back_tick,
            send_ffn,
            send_attn,
        )
    flat = jnp.concatenate([jnp.stack(norm_parts).reshape(-1), jnp.stack(head_parts).reshape(-1)])
    gains_sum = Transfer(sum_all(flat.reshape(-1, 128)))
    sums.append(gains_sum)
    while any(move.flying is not None for move in sums):
        advance((), sums)
    upstream = exchange_rows(upstream.astype(jnp.bfloat16)).astype(jnp.float32)
    weight_shares = []
    for layer_idx in range(layer_count):
        ffn_total = ffn_sums[layer_idx].result
        weight_shares.append(
            attn_shares(attn_sums[layer_idx].result, attn_rows[layer_idx])
            + [ffn_total[kind] for kind in range(3)]
        )
    both = gains_sum.result.reshape(-1)
    norm_total = both[: norm_gains.size].reshape(norm_gains.shape)
    head_total = both[norm_gains.size :].reshape(head_gains.shape)
    stacked = tuple(
        (
            jnp.stack([weight_shares[layer_idx][member] for layer_idx in range(layer_count)])
            for member in range(7)
        )
    )
    return (block_out, upstream) + stacked + (norm_total, head_total)


def solution(mesh):
    in_specs = (
        P("wsh", "seq", None),
        P("wsh", "seq"),
        P(None, ("seq", "wsh"), None),
        P(None, ("seq", "wsh"), None),
        P(None, ("seq", "wsh"), None),
        P(None, ("seq", "wsh"), None),
        P(None, ("seq", "wsh"), None),
        P(None, ("seq", "wsh"), None),
        P(None, ("seq", "wsh"), None),
        P(),
        P(),
        P("wsh", "seq", None),
    )
    out_specs = (
        P("wsh", "seq", None),
        P("wsh", "seq", None),
        P(None, ("seq", "wsh"), None),
        P(None, ("seq", "wsh"), None),
        P(None, ("seq", "wsh"), None),
        P(None, ("seq", "wsh"), None),
        P(None, ("seq", "wsh"), None),
        P(None, ("seq", "wsh"), None),
        P(None, ("seq", "wsh"), None),
        P(),
        P(),
    )
    return jax.shard_map(body, mesh=mesh, in_specs=in_specs, out_specs=out_specs, check_vma=False)
```
